128 devices in a mesh: layer: 4 (over y), row: 4 (over x_hi, core), col: 8 (over x_lo, z).
Axes of the slice: x: 4 (x_hi: 2, x_lo: 2; x = x_hi * 2 + x_lo), y: 4, z: 4, core: 2. Of those that a mesh axis runs over, the one named last changes fastest.
Arguments:
- t2_slab: bfloat16 [16384, 4096], P('row', ('layer', 'col')), may hold values from -0.1875 to 0.1875
- lambda_block: bfloat16 [4096, 16384], P(('layer', 'row'), 'col'), may hold values from -6 to 6
Outputs:
- density_panel: bfloat16 [16384, 16384], P(('row', 'layer'), 'col')
The draws below stay inside these ranges and needn't reach their ends.
All inputs are finite; a program needn't handle non-finite values.
Results may differ from the reference program's by a relative error of at most 0.015.
Values may be sent and summed in bfloat16 or wider, within the bound.
No kernel may reach another device: no remote copies, remote signals or barrier semaphores. Data moves between devices by JAX's collectives and lax.ppermute only.
A program may use at most 128 MiB of HBM per device.

```python
import jax
import jax.numpy as jnp

PANEL_ROWS = 16384
SLAB = 4096
PANEL_COLS = 16384


def raised(entries, key, source, target, parts, factor):
    owner, partner = [(jnp.arange(entries.shape[position]) // (entries.shape[position] // parts)).reshape([-1 if axis == position else 1 for axis in range(entries.ndim)]) for position in (source, target)]
    chosen = jax.random.permutation(key, parts)[partner]
    strong = (owner == chosen) | (owner == (partner + parts // 2) % parts)
    return jnp.where(strong, factor * entries, entries)


def levels(stream_key, dims, cuts, smallest, top_value):
    loudness = 1.0
    for axis_at, blocks in cuts:
        draws = jax.random.uniform(jax.random.fold_in(jax.random.fold_in(stream_key, 6), axis_at), (blocks,), jnp.float32, smallest / len(cuts), top_value / len(cuts))
        loudness = loudness * jnp.repeat(jnp.exp(draws), dims[axis_at] // blocks).reshape((-1,) + (1,) * (len(dims) - 1 - axis_at))
    return loudness


def normal_values(key, dims, scale, most, cuts=(), dtype=jnp.bfloat16):
    values = scale * jax.random.normal(key, dims, jnp.float32)
    if cuts:
        values = values * levels(key, dims, cuts, -0.22, 0.18)
    return jnp.clip(values, -most, most).astype(dtype)


def heavy_noise(key, shape, spread, most, cuts, heavy, kind=jnp.bfloat16):
    values = spread * jax.random.normal(key, shape, jnp.float32)
    if cuts:
        values = values * levels(key, shape, cuts, -0.22, 0.18)
    return jnp.clip(raised(values, jax.random.fold_in(key, 3), *heavy), -most, most).astype(kind)


def setup_inputs(seed: int = 0) -> dict:
    splits = jax.random.split(jax.random.key(seed), 3)
    return {
        "t2_slab": heavy_noise(splits[0], (PANEL_ROWS, SLAB), SLAB ** -0.5, 0.1875, ((0, 4), (1, 32)), (1, 0, 32, 2.75)),
        "lambda_block": normal_values(splits[1], (SLAB, PANEL_COLS), 1.0, 6.0, ((0, 16), (1, 8))),
    }


def reference(t2_slab, lambda_block):
    cycle_sum = jnp.dot(t2_slab, lambda_block, preferred_element_type=jnp.float32)
    return cycle_sum.astype(jnp.bfloat16)
```

```python
import functools

import jax
import jax.numpy as jnp
from jax import lax
from jax.experimental import pallas as pl
from jax.experimental.pallas import tpu as pltpu
from jax.sharding import PartitionSpec as P

AXES = ("layer", "row", "col")
TILE = 256


def flat(y, xh, c, xl, z):
    return (y % 4 * 4 + xh % 2 * 2 + c % 2) * 8 + xl % 2 * 4 + z % 4


def pairs(move):
    return [
        (flat(y, xh, c, xl, z), flat(*move(y, xh, c, xl, z)))
        for y in range(4) for xh in range(2) for c in range(2) for xl in range(2) for z in range(4)
    ]


def way(c):
    return 1 if c == 0 else -1


Y_RING = pairs(lambda y, xh, c, xl, z: (y + way(c), xh, c, xl, z))
Y_BACK = pairs(lambda y, xh, c, xl, z: (y - way(c), xh, c, xl, z))
Y_FAR = pairs(lambda y, xh, c, xl, z: (y + 2, xh, c, xl, z))
Z_RING = pairs(lambda y, xh, c, xl, z: (y, xh, c, xl, z + way(c)))
XH = pairs(lambda y, xh, c, xl, z: (y, xh + 1, c, xl, z))
XL = pairs(lambda y, xh, c, xl, z: (y, xh, c, xl + 1, z))
CORE = pairs(lambda y, xh, c, xl, z: (y, xh, c + 1, xl, z))


def send(x, perm):
    return lax.ppermute(x, AXES, perm)


def multiply_kernel(places, n_a, n_b, has_acc, place_ref, *refs):
    a_refs, b_refs = refs[:n_a], refs[n_a : n_a + n_b]
    refs = refs[n_a + n_b :]
    acc_ref = refs[0] if has_acc else None
    out_ref, lhs, rhs, sems = refs[has_acc:]

    @pl.when(pl.program_id(0) == 0)
    def _():
        copies = []
        for i, (array, part) in enumerate(places):
            to = pl.ds(pl.multiple_of(place_ref[i] * 128, 128), 128)
            copies.append(pltpu.make_async_copy(a_refs[array].at[part], lhs.at[:, to], sems.at[i]))
        for i in range(n_b):
            to = pl.ds(pl.multiple_of(place_ref[len(places) + i] * 256, 256), 256)
            copies.append(pltpu.make_async_copy(b_refs[i], rhs.at[to], sems.at[len(places) + i]))
        for copy in copies:
            copy.start()
        for copy in copies:
            copy.wait()

    columns = pl.ds(pl.multiple_of(pl.program_id(0) * TILE, TILE), TILE)
    total = jnp.dot(lhs[:, :1024], rhs[:, columns], preferred_element_type=jnp.float32)
    if has_acc:
        total += acc_ref[...]
    out_ref[...] = total.astype(out_ref.dtype)


def multiply(acc, pieces, a_places, b_pieces, b_places, dtype):
    arrays, places = [], []
    for array, part in pieces:
        at = next((i for i, other in enumerate(arrays) if other is array), None)
        if at is None:
            at = len(arrays)
            arrays.append(array)
        places.append((at, part))
    n_a, n_b, has_acc = len(arrays), len(b_pieces), int(acc is not None)
    anywhere = pl.BlockSpec(memory_space=pl.ANY)
    tile = pl.BlockSpec((1024, TILE), lambda j, *_: (0, j))
    kernel = functools.partial(multiply_kernel, tuple(places), n_a, n_b, has_acc)
    return pl.pallas_call(
        kernel,
        grid_spec=pltpu.PrefetchScalarGridSpec(
            num_scalar_prefetch=1,
            grid=(2048 // TILE,),
            in_specs=[anywhere] * (n_a + n_b) + [tile] * has_acc,
            out_specs=tile,
            scratch_shapes=[
                pltpu.VMEM((1024, 2048), jnp.bfloat16),
                pltpu.VMEM((1024, 2048), jnp.bfloat16),
                pltpu.SemaphoreType.DMA((len(places) + n_b,)),
            ],
        ),
        out_shape=jax.ShapeDtypeStruct((1024, 2048), dtype),
        compiler_params=pltpu.CompilerParams(vmem_limit_bytes=32 * 2**20),
        cost_estimate=pl.CostEstimate(flops=2 * 1024 * 1024 * 2048, bytes_accessed=24 * 2**20, transcendentals=0),
    )(jnp.stack(a_places + b_places).astype(jnp.int32), *arrays, *b_pieces, *([acc] * has_acc))


def local(t2_slab, lambda_block):
    y, row, col = (lax.axis_index(a) for a in AXES)
    xh, c, xl, z = row // 2, row % 2, col // 4, col % 4
    sgn = 2 * c - 1

    def block(at):
        return lax.dynamic_slice(t2_slab, (lax.rem(at + 8, 4) * 1024, 0), (1024, 128))[None]

    a0 = block(y)
    a1 = send(block(y - sgn), Y_RING)
    a3 = send(block(y + sgn), Y_BACK)
    a2 = send(block(y + 2), Y_FAR)
    o0 = send(a0, XL)
    rest = jnp.concatenate([a1, a2, a3])
    o_rest = send(rest, XL)
    groups = [a0, jnp.concatenate([o0, rest]), o_rest]
    where = {(0, 0): (0, 0), (0, 1): (1, 0)}
    for t in (1, 2, 3):
        where[t, 0], where[t, 1] = (1, t), (2, t - 1)
    steps = [groups]
    for _ in range(3):
        steps.append([send(g, Z_RING) for g in steps[-1]])

    b = [lambda_block]
    for _ in range(3):
        b.append(send(b[-1], Y_RING))
    p = [send(b[0], XH)]
    for _ in range(2):
        p.append(send(p[-1], Y_RING))
    p.append(send(b[3], XH))

    acc = None
    for s in (0, 2, 1, 3):
        pieces, a_places = [], []
        for t in sorted({s, -s % 4}):
            for other in (0, 1):
                h = jnp.abs(xl - other)
                for r in range(4):
                    group, part = where[t, other]
                    pieces.append((steps[r][group], part))
                    zz = lax.rem(z + r * sgn + 8, 4)
                    half = jnp.abs(zz // 2 - c)
                    at = h * 4 + half * 2 + zz % 2
                    if s % 2:
                        at = at + 8 * (half if t == s else 1 - half)
                    a_places.append(at)
        swapped = [send(v, CORE) for v in (b[s], p[s])]
        b_pieces = [b[s], p[s], *swapped]
        b_places = [xh * 2, (1 - xh) * 2, xh * 2 + 1, (1 - xh) * 2 + 1]
        acc = multiply(acc, pieces, a_places, b_pieces, b_places, jnp.bfloat16 if s == 3 else jnp.float32)
    return acc


def solution(mesh):
    placed = (P("row", ("layer", "col")), P(("layer", "row"), "col"))
    return jax.shard_map(
        local, mesh=mesh, in_specs=placed, out_specs=P(("row", "layer"), "col"), check_vma=False
    )
```

```python
import functools

import jax
import jax.numpy as jnp
from jax import lax
from jax.experimental import pallas as pl
from jax.experimental.pallas import tpu as pltpu
from jax.sharding import PartitionSpec as P

AXES = ("layer", "row", "col")
SPAN = 512


def flat(y, xh, c, xl, z):
    return (y % 4 * 4 + xh % 2 * 2 + c % 2) * 8 + xl % 2 * 4 + z % 4


def pairs(move):
    return [
        (flat(y, xh, c, xl, z), flat(*move(y, xh, c, xl, z)))
        for y in range(4) for xh in range(2) for c in range(2) for xl in range(2) for z in range(4)
    ]


def way(c):
    return 1 if c == 0 else -1


Y_RING = pairs(lambda y, xh, c, xl, z: (y + way(c), xh, c, xl, z))
Y_BACK = pairs(lambda y, xh, c, xl, z: (y - way(c), xh, c, xl, z))
Y_FAR = pairs(lambda y, xh, c, xl, z: (y + 2, xh, c, xl, z))
Z_RING = pairs(lambda y, xh, c, xl, z: (y, xh, c, xl, z + way(c)))
Z_BACK = pairs(lambda y, xh, c, xl, z: (y, xh, c, xl, z - way(c)))
XH = pairs(lambda y, xh, c, xl, z: (y, xh + 1, c, xl, z))
XL = pairs(lambda y, xh, c, xl, z: (y, xh, c, xl + 1, z))
CORE = pairs(lambda y, xh, c, xl, z: (y, xh, c + 1, xl, z))

STEPS = (
    ("A1", ("k1",), Y_RING, ()),
    ("A3", ("k3",), Y_BACK, ()),
    ("A2", ("k2",), Y_FAR, ()),
    ("O0", ("k0",), XL, ()),
    ("P0", ("b0",), XH, ()),
    ("X123", ("A1", "A3", "A2"), XL, ()),
    ("B3", ("b0",), Y_BACK, ()),
    ("B1", ("b0",), Y_RING, ()),
    ("B2", ("B1",), Y_RING, ()),
    ("n0", ("k0", "O0", "A1", "A3"), Z_RING, ()),
    ("c0", ("k0", "O0", "A1", "A3"), Z_BACK, ()),
    ("f0", ("n0",), Z_RING, ()),
    ("c1", ("A2", "X123"), Z_BACK, ()),
    ("Cb0", ("b0",), CORE, ()),
    ("CP0", ("P0",), CORE, ()),
    ("CB3", ("B3",), CORE, ()),
    ("M0", (0,), 0.01, ()),
    ("Q1", ("P0",), Y_RING, ("c0",)),
    ("Q2", ("Q1",), Y_RING, ("f0", "X123", "A2")),
    ("P3", ("B3",), XH, ("n0",)),
    ("n1", ("A2", "X123"), Z_RING, ("CB3",)),
    ("f1", ("n1",), Z_RING, ()),
    ("CB1", ("B1",), CORE, ("M0", "O0")),
    ("CQ1", ("Q1",), CORE, ()),
    ("CB2", ("B2",), CORE, ("Q2",)),
    ("CQ2", ("Q2",), CORE, ("f1", "c1")),
    ("CP3", ("P3",), CORE, ("M0", "A2")),
    ("M1", (1, 3,), 1, ()),
    ("M2", (2,), 10, ()),
)
GROUPS = (
    ("k0", "O0", "A1", "A3"),
    ("A2", "X123"),
)
WHERE = {
    (0, 0): (0, 0),
    (0, 1): (0, 1),
    (1, 0): (0, 2),
    (1, 1): (1, 1),
    (2, 0): (1, 0),
    (2, 1): (1, 3),
    (3, 0): (0, 3),
    (3, 1): (1, 2),
}
ROWS = (
    (("b0",), ("P0",), ("Cb0",), ("CP0",)),
    (("B1",), ("Q1",), ("CB1",), ("CQ1",)),
    (("B2",), ("Q2",), ("CB2",), ("CQ2",)),
    (("B3",), ("P3",), ("CB3",), ("CP3",)),
)


def kernel(tile, places, n_a, n_b, has_acc, place_ref, *refs):
    a_refs, b_refs = refs[:n_a], refs[n_a : n_a + n_b]
    refs = refs[n_a + n_b :]
    acc_ref = refs[0] if has_acc else None
    out_ref, lhs, sems = refs[has_acc:]
    first = pl.program_id(0) == 0

    def copies(top):
        rows = pl.ds(top, SPAN)
        return [
            pltpu.make_async_copy(
                a_refs[array].at[part, rows], lhs.at[place_ref[i], rows], sems.at[i, top // SPAN]
            )
            for i, (array, part) in enumerate(places)
        ]

    @pl.when(first)
    def _():
        for top in range(0, 1024, SPAN):
            for copy in copies(top):
                copy.start()

    rhs = jnp.concatenate([ref[...].reshape(-1, tile) for ref in b_refs], axis=0)
    for top in range(0, 1024, SPAN):

        @pl.when(first)
        def _():
            for copy in copies(top):
                copy.wait()

        for at in range(top, top + SPAN, 256):
            rows = slice(at, at + 256)
            left = jnp.concatenate([lhs[i, rows, :] for i in range(rhs.shape[0] // 128)], axis=1)
            total = jnp.dot(left, rhs, preferred_element_type=jnp.float32)
            if has_acc:
                total += acc_ref[rows, :].astype(jnp.float32)
            out_ref[rows, :] = total.astype(out_ref.dtype)


def multiply(acc, pieces, slots, n_slots, b_arrays, weight):
    arrays, places = [], []
    for array, part in pieces:
        at = next((i for i, other in enumerate(arrays) if other is array), None)
        if at is None:
            at = len(arrays)
            arrays.append(array)
        places.append((at, part))
    n_a, n_b, has_acc = len(arrays), len(b_arrays), int(acc is not None)
    depth = sum(b.shape[0] * b.shape[1] for b in b_arrays)
    tile = 512 if depth < 3000 else 256
    anywhere = pl.BlockSpec(memory_space=pl.ANY)
    columns = pl.BlockSpec((1024, tile), lambda j, *_: (0, j))
    return pl.pallas_call(
        functools.partial(kernel, tile, tuple(places), n_a, n_b, has_acc),
        grid_spec=pltpu.PrefetchScalarGridSpec(
            num_scalar_prefetch=1,
            grid=(2048 // tile,),
            in_specs=[anywhere] * n_a
            + [pl.BlockSpec((*b.shape[:2], tile), lambda j, *_: (0, 0, j)) for b in b_arrays]
            + [columns] * has_acc,
            out_specs=columns,
            scratch_shapes=[
                pltpu.VMEM((n_slots, 1024, 128), jnp.bfloat16),
                pltpu.SemaphoreType.DMA((len(places), 1024 // SPAN)),
            ],
        ),
        out_shape=jax.ShapeDtypeStruct((1024, 2048), jnp.bfloat16),
        compiler_params=pltpu.CompilerParams(vmem_limit_bytes=50 * 2**20),
        cost_estimate=pl.CostEstimate(
            flops=int(2 * 1024 * depth * 2048 * weight),
            bytes_accessed=int(20 * 2**20 * weight),
            transcendentals=0,
        ),
    )(jnp.stack(slots).astype(jnp.int32), *arrays, *b_arrays, *([acc] * has_acc))


def local(t2_slab, lambda_block):
    y, row, col = (lax.axis_index(a) for a in AXES)
    xh, c, xl, z = row // 2, row % 2, col // 4, col % 4
    sgn = 2 * c - 1

    def block(layer):
        return lax.dynamic_slice(t2_slab, (lax.rem(layer + 8, 4) * 1024, 0), (1024, 128))[None]

    held = {"k0": block(y), "k1": block(y - sgn), "k3": block(y + sgn), "k2": block(y + 2)}
    held["b0"] = lambda_block[None]
    joined = {}

    def join(names):
        if names not in joined:
            blocks = [held[name] for name in names]
            joined[names] = blocks[0] if len(blocks) == 1 else jnp.concatenate(blocks)
        return joined[names]

    def product(acc, distances, weight):
        base = {s: 8 * i for i, s in enumerate(distances)}
        spare, spared = 8 * len(distances), False
        pieces, slots = [], []
        for t in sorted({t for s in distances for t in (s, -s % 4)}):
            mine, theirs = base.get(t, spare), base.get(-t % 4, spare)
            spared |= spare in (mine, theirs)
            for other in (0, 1):
                group, part = WHERE[t, other]
                steps = [join(GROUPS[group])] + [held[f"{step}{group}"] for step in "nfc"]
                for r in range(4):
                    zz = lax.rem(z + r * sgn + 8, 4)
                    away = jnp.abs(zz // 2 - c)
                    apart = jnp.abs(jnp.abs(xl - other) - xh)
                    pieces.append((steps[r], part))
                    slots.append(mine + away * (theirs - mine) + away * 4 + apart * 2 + zz % 2)
        b_arrays = [join(names) for s in distances for names in ROWS[s]]
        return multiply(acc, pieces, slots, spare + 8 * spared, b_arrays, weight)

    acc = None
    for name, what, how, wait in STEPS:
        if isinstance(how, list):
            sent = join(what)
            if wait:
                sent = lax.optimization_barrier((sent, *(held[other] for other in wait)))[0]
            held[name] = lax.ppermute(sent, AXES, how)
        else:
            acc = held[name] = product(acc, what, how)
    return acc


def solution(mesh):
    placed = (P("row", ("layer", "col")), P(("layer", "row"), "col"))
    return jax.shard_map(
        local, mesh=mesh, in_specs=placed, out_specs=P(("row", "layer"), "col"), check_vma=False
    )
```

```python
import functools

import jax
import jax.numpy as jnp
from jax import lax
from jax.experimental import pallas as pl
from jax.experimental.pallas import tpu as pltpu
from jax.sharding import PartitionSpec as P

AXES = ("layer", "row", "col")
SPAN = 1024


def flat(y, xh, c, xl, z):
    return (y % 4 * 4 + xh % 2 * 2 + c % 2) * 8 + xl % 2 * 4 + z % 4


def pairs(move):
    return [
        (flat(y, xh, c, xl, z), flat(*move(y, xh, c, xl, z)))
        for y in range(4) for xh in range(2) for c in range(2) for xl in range(2) for z in range(4)
    ]


def way(c):
    return 1 if c == 0 else -1


Y_RING = pairs(lambda y, xh, c, xl, z: (y + way(c), xh, c, xl, z))
Y_BACK = pairs(lambda y, xh, c, xl, z: (y - way(c), xh, c, xl, z))
Y_FAR = pairs(lambda y, xh, c, xl, z: (y + 2, xh, c, xl, z))
Z_RING = pairs(lambda y, xh, c, xl, z: (y, xh, c, xl, z + way(c)))
Z_BACK = pairs(lambda y, xh, c, xl, z: (y, xh, c, xl, z - way(c)))
XH = pairs(lambda y, xh, c, xl, z: (y, xh + 1, c, xl, z))
XL = pairs(lambda y, xh, c, xl, z: (y, xh, c, xl + 1, z))
CORE = pairs(lambda y, xh, c, xl, z: (y, xh, c + 1, xl, z))

STEPS = (
    ("A1", ("k1",), Y_RING, ()),
    ("A3", ("k3",), Y_BACK, ()),
    ("O0", ("k0",), XL, ()),
    ("P0", ("b0",), XH, ()),
    ("B3", ("b0",), Y_BACK, ()),
    ("n0", ("k0", "O0", "A1", "A3"), Z_RING, ()),
    ("c0", ("k0", "O0", "A1", "A3"), Z_BACK, ()),
    ("f0", ("n0",), Z_RING, ()),
    ("Cb0", ("b0",), CORE, ()),
    ("CP0", ("P0",), CORE, ()),
    ("CB3", ("B3",), CORE, ()),
    ("M0", (0,), 0.01, ()),
    ("A2", ("k2",), Y_FAR, ("O0",)),
    ("X123", ("A1", "A3", "A2"), XL, ()),
    ("B1", ("b0",), Y_RING, ("A2",)),
    ("B2", ("B1",), Y_RING, ()),
    ("Q1", ("P0",), Y_RING, ("c0",)),
    ("Q2", ("Q1",), Y_RING, ("f0", "X123", "A2")),
    ("P3", ("B3",), XH, ("n0",)),
    ("n1", ("A2", "X123"), Z_RING, ("CB3",)),
    ("c1", ("A2", "X123"), Z_BACK, ()),
    ("f1", ("n1",), Z_RING, ()),
    ("CB1", ("B1",), CORE, ("M0",)),
    ("CQ1", ("Q1",), CORE, ()),
    ("CB2", ("B2",), CORE, ("Q2", "f0", "A2")),
    ("CQ2", ("Q2",), CORE, ("f1", "c1")),
    ("CP3", ("P3",), CORE, ("M0", "A2")),
    ("M1", (1, 3,), 1, ()),
    ("M2", (2,), 3, ()),
)
GROUPS = (
    ("k0", "O0", "A1", "A3"),
    ("A2", "X123"),
)
WHERE = {
    (0, 0): (0, 0),
    (0, 1): (0, 1),
    (1, 0): (0, 2),
    (1, 1): (1, 1),
    (2, 0): (1, 0),
    (2, 1): (1, 3),
    (3, 0): (0, 3),
    (3, 1): (1, 2),
}
ROWS = (
    (("b0",), ("P0",), ("Cb0",), ("CP0",)),
    (("B1",), ("Q1",), ("CB1",), ("CQ1",)),
    (("B2",), ("Q2",), ("CB2",), ("CQ2",)),
    (("B3",), ("P3",), ("CB3",), ("CP3",)),
)


def kernel(tile, places, n_a, n_b, has_acc, place_ref, *refs):
    a_refs, b_refs = refs[:n_a], refs[n_a : n_a + n_b]
    refs = refs[n_a + n_b :]
    acc_ref = refs[0] if has_acc else None
    out_ref, lhs, sems = refs[has_acc:]
    first = pl.program_id(0) == 0

    def copies(top):
        rows = pl.ds(top, SPAN)
        return [
            pltpu.make_async_copy(
                a_refs[array].at[part, rows], lhs.at[place_ref[i], rows], sems.at[i, top // SPAN]
            )
            for i, (array, part) in enumerate(places)
        ]

    @pl.when(first)
    def _():
        for top in range(0, 1024, SPAN):
            for copy in copies(top):
                copy.start()

    rhs = jnp.concatenate([ref[...].reshape(-1, tile) for ref in b_refs], axis=0)
    for top in range(0, 1024, SPAN):

        @pl.when(first)
        def _():
            for copy in copies(top):
                copy.wait()

        for at in range(top, top + SPAN, 256):
            rows = slice(at, at + 256)
            left = jnp.concatenate([lhs[i, rows, :] for i in range(rhs.shape[0] // 128)], axis=1)
            total = jnp.dot(left, rhs, preferred_element_type=jnp.float32)
            if has_acc:
                total += acc_ref[rows, :].astype(jnp.float32)
            out_ref[rows, :] = total.astype(out_ref.dtype)


def multiply(acc, pieces, slots, n_slots, b_arrays, weight):
    arrays, places = [], []
    for array, part in pieces:
        at = next((i for i, other in enumerate(arrays) if other is array), None)
        if at is None:
            at = len(arrays)
            arrays.append(array)
        places.append((at, part))
    n_a, n_b, has_acc = len(arrays), len(b_arrays), int(acc is not None)
    depth = sum(b.shape[0] * b.shape[1] for b in b_arrays)
    tile = 512 if depth < 3000 else 256
    anywhere = pl.BlockSpec(memory_space=pl.ANY)
    columns = pl.BlockSpec((1024, tile), lambda j, *_: (0, j))
    return pl.pallas_call(
        functools.partial(kernel, tile, tuple(places), n_a, n_b, has_acc),
        grid_spec=pltpu.PrefetchScalarGridSpec(
            num_scalar_prefetch=1,
            grid=(2048 // tile,),
            in_specs=[anywhere] * n_a
            + [pl.BlockSpec((*b.shape[:2], tile), lambda j, *_: (0, 0, j)) for b in b_arrays]
            + [columns] * has_acc,
            out_specs=columns,
            scratch_shapes=[
                pltpu.VMEM((n_slots, 1024, 128), jnp.bfloat16),
                pltpu.SemaphoreType.DMA((len(places), 1024 // SPAN)),
            ],
        ),
        out_shape=jax.ShapeDtypeStruct((1024, 2048), jnp.bfloat16),
        compiler_params=pltpu.CompilerParams(vmem_limit_bytes=50 * 2**20),
        cost_estimate=pl.CostEstimate(
            flops=int(2 * 1024 * depth * 2048 * weight),
            bytes_accessed=int(20 * 2**20 * weight),
            transcendentals=0,
        ),
    )(jnp.stack(slots).astype(jnp.int32), *arrays, *b_arrays, *([acc] * has_acc))


def local(t2_slab, lambda_block):
    y, row, col = (lax.axis_index(a) for a in AXES)
    xh, c, xl, z = row // 2, row % 2, col // 4, col % 4
    sgn = 2 * c - 1

    def block(layer):
        return lax.dynamic_slice(t2_slab, (lax.rem(layer + 8, 4) * 1024, 0), (1024, 128))[None]

    held = {"k0": block(y), "k1": block(y - sgn), "k3": block(y + sgn), "k2": block(y + 2)}
    held["b0"] = lambda_block[None]
    joined = {}

    def join(names):
        if names not in joined:
            blocks = [held[name] for name in names]
            joined[names] = blocks[0] if len(blocks) == 1 else jnp.concatenate(blocks)
        return joined[names]

    def product(acc, distances, weight):
        base = {s: 8 * i for i, s in enumerate(distances)}
        spare, spared = 8 * len(distances), False
        pieces, slots = [], []
        for t in sorted({t for s in distances for t in (s, -s % 4)}):
            mine, theirs = base.get(t, spare), base.get(-t % 4, spare)
            spared |= spare in (mine, theirs)
            for other in (0, 1):
                group, part = WHERE[t, other]
                steps = [join(GROUPS[group])] + [held[f"{step}{group}"] for step in "nfc"]
                for r in range(4):
                    zz = lax.rem(z + r * sgn + 8, 4)
                    away = jnp.abs(zz // 2 - c)
                    apart = jnp.abs(jnp.abs(xl - other) - xh)
                    pieces.append((steps[r], part))
                    slots.append(mine + away * (theirs - mine) + away * 4 + apart * 2 + zz % 2)
        b_arrays = [join(names) for s in distances for names in ROWS[s]]
        return multiply(acc, pieces, slots, spare + 8 * spared, b_arrays, weight)

    acc = None
    for name, what, how, wait in STEPS:
        if isinstance(how, list):
            sent = join(what)
            if wait:
                sent = lax.optimization_barrier((sent, *(held[other] for other in wait)))[0]
            held[name] = lax.ppermute(sent, AXES, how)
        else:
            acc = held[name] = product(acc, what, how)
    return acc


def solution(mesh):
    placed = (P("row", ("layer", "col")), P(("layer", "row"), "col"))
    return jax.shard_map(
        local, mesh=mesh, in_specs=placed, out_specs=P(("row", "layer"), "col"), check_vma=False
    )
```

```python
import functools

import jax
import jax.numpy as jnp
from jax import lax
from jax.experimental import pallas as pl
from jax.experimental.pallas import tpu as pltpu
from jax.sharding import PartitionSpec as P

AXES = ("layer", "row", "col")
SPAN = 1024


def flat(y, xh, c, xl, z):
    return (y % 4 * 4 + xh % 2 * 2 + c % 2) * 8 + xl % 2 * 4 + z % 4


def pairs(move):
    return [
        (flat(y, xh, c, xl, z), flat(*move(y, xh, c, xl, z)))
        for y in range(4) for xh in range(2) for c in range(2) for xl in range(2) for z in range(4)
    ]


def way(c):
    return 1 if c == 0 else -1


Y_RING = pairs(lambda y, xh, c, xl, z: (y + way(c), xh, c, xl, z))
Y_BACK = pairs(lambda y, xh, c, xl, z: (y - way(c), xh, c, xl, z))
Y_FAR = pairs(lambda y, xh, c, xl, z: (y + 2, xh, c, xl, z))
Z_RING = pairs(lambda y, xh, c, xl, z: (y, xh, c, xl, z + way(c)))
Z_BACK = pairs(lambda y, xh, c, xl, z: (y, xh, c, xl, z - way(c)))
XH = pairs(lambda y, xh, c, xl, z: (y, xh + 1, c, xl, z))
XL = pairs(lambda y, xh, c, xl, z: (y, xh, c, xl + 1, z))
CORE = pairs(lambda y, xh, c, xl, z: (y, xh, c + 1, xl, z))

STEPS = (
    ("A1", ("k1",), Y_RING, ()),
    ("A3", ("k3",), Y_BACK, ()),
    ("O0", ("k0",), XL, ()),
    ("P0", ("b0",), XH, ()),
    ("B3", ("b0",), Y_BACK, ()),
    ("n0", ("k0", "O0", "A1", "A3"), Z_RING, ()),
    ("c0", ("k0", "O0", "A1", "A3"), Z_BACK, ()),
    ("f0", ("n0",), Z_RING, ()),
    ("Cb0", ("b0",), CORE, ()),
    ("CP0", ("P0",), CORE, ()),
    ("CB3", ("B3",), CORE, ()),
    ("M0", (0,), 0.01, ()),
    ("A2", ("k2",), Y_FAR, ("O0",)),
    ("X123", ("A1", "A3", "A2"), XL, ()),
    ("B1", ("b0",), Y_RING, ("A2",)),
    ("B2", ("B1",), Y_RING, ()),
    ("Q1", ("P0",), Y_RING, ("c0",)),
    ("Q2", ("Q1",), Y_RING, ("f0", "X123", "A2")),
    ("P3", ("B3",), XH, ("n0",)),
    ("n1", ("A2", "X123"), Z_RING, ("CB3",)),
    ("c1", ("A2", "X123"), Z_BACK, ()),
    ("f1", ("n1",), Z_RING, ()),
    ("CB1", ("B1",), CORE, ("M0",)),
    ("CQ1", ("Q1",), CORE, ()),
    ("CB2", ("B2",), CORE, ("Q2", "f0", "A2")),
    ("CQ2", ("Q2",), CORE, ("f1", "c1")),
    ("CP3", ("P3",), CORE, ("M0", "A2")),
    ("M1", (1, 3,), 1, ()),
    ("M2", (2,), 3, ()),
)
GROUPS = (
    ("k0", "O0", "A1", "A3"),
    ("A2", "X123"),
)
WHERE = {
    (0, 0): (0, 0),
    (0, 1): (0, 1),
    (1, 0): (0, 2),
    (1, 1): (1, 1),
    (2, 0): (1, 0),
    (2, 1): (1, 3),
    (3, 0): (0, 3),
    (3, 1): (1, 2),
}
ROWS = (
    (("b0",), ("P0",), ("Cb0",), ("CP0",)),
    (("B1",), ("Q1",), ("CB1",), ("CQ1",)),
    (("B2",), ("Q2",), ("CB2",), ("CQ2",)),
    (("B3",), ("P3",), ("CB3",), ("CP3",)),
)


def kernel(tile, places, n_a, n_b, has_acc, place_ref, *refs):
    a_refs, b_refs = refs[:n_a], refs[n_a : n_a + n_b]
    refs = refs[n_a + n_b :]
    acc_ref = refs[0] if has_acc else None
    out_ref, lhs, sems = refs[has_acc:]
    first = pl.program_id(0) == 0

    def copies(top):
        rows = pl.ds(top, SPAN)
        return [
            pltpu.make_async_copy(
                a_refs[array].at[part, rows], lhs.at[place_ref[i], rows], sems.at[i, top // SPAN]
            )
            for i, (array, part) in enumerate(places)
        ]

    @pl.when(first)
    def _():
        for top in range(0, 1024, SPAN):
            for i, copy in enumerate(copies(top)):
                copy.start(priority=i % 2)

    rhs = jnp.concatenate([ref[...].reshape(-1, tile) for ref in b_refs], axis=0)
    for top in range(0, 1024, SPAN):

        @pl.when(first)
        def _():
            for copy in copies(top):
                copy.wait()

        for at in range(top, top + SPAN, 256):
            rows = slice(at, at + 256)
            left = jnp.concatenate([lhs[i, rows, :] for i in range(rhs.shape[0] // 128)], axis=1)
            total = jnp.dot(left, rhs, preferred_element_type=jnp.float32)
            if has_acc:
                total += acc_ref[rows, :].astype(jnp.float32)
            out_ref[rows, :] = total.astype(out_ref.dtype)


def multiply(acc, pieces, slots, n_slots, b_arrays, weight):
    arrays, places = [], []
    for array, part in pieces:
        at = next((i for i, other in enumerate(arrays) if other is array), None)
        if at is None:
            at = len(arrays)
            arrays.append(array)
        places.append((at, part))
    n_a, n_b, has_acc = len(arrays), len(b_arrays), int(acc is not None)
    depth = sum(b.shape[0] * b.shape[1] for b in b_arrays)
    tile = 512 if depth < 3000 else 256
    anywhere = pl.BlockSpec(memory_space=pl.ANY)
    columns = pl.BlockSpec((1024, tile), lambda j, *_: (0, j))
    return pl.pallas_call(
        functools.partial(kernel, tile, tuple(places), n_a, n_b, has_acc),
        grid_spec=pltpu.PrefetchScalarGridSpec(
            num_scalar_prefetch=1,
            grid=(2048 // tile,),
            in_specs=[anywhere] * n_a
            + [pl.BlockSpec((*b.shape[:2], tile), lambda j, *_: (0, 0, j)) for b in b_arrays]
            + [columns] * has_acc,
            out_specs=columns,
            scratch_shapes=[
                pltpu.VMEM((n_slots, 1024, 128), jnp.bfloat16),
                pltpu.SemaphoreType.DMA((len(places), 1024 // SPAN)),
            ],
        ),
        out_shape=jax.ShapeDtypeStruct((1024, 2048), jnp.bfloat16),
        compiler_params=pltpu.CompilerParams(vmem_limit_bytes=50 * 2**20),
        cost_estimate=pl.CostEstimate(
            flops=int(2 * 1024 * depth * 2048 * weight),
            bytes_accessed=int(20 * 2**20 * weight),
            transcendentals=0,
        ),
    )(jnp.stack(slots).astype(jnp.int32), *arrays, *b_arrays, *([acc] * has_acc))


def local(t2_slab, lambda_block):
    y, row, col = (lax.axis_index(a) for a in AXES)
    xh, c, xl, z = row // 2, row % 2, col // 4, col % 4
    sgn = 2 * c - 1

    def block(layer):
        return lax.dynamic_slice(t2_slab, (lax.rem(layer + 8, 4) * 1024, 0), (1024, 128))[None]

    held = {"k0": block(y), "k1": block(y - sgn), "k3": block(y + sgn), "k2": block(y + 2)}
    held["b0"] = lambda_block[None]
    joined = {}

    def join(names):
        if names not in joined:
            blocks = [held[name] for name in names]
            joined[names] = blocks[0] if len(blocks) == 1 else jnp.concatenate(blocks)
        return joined[names]

    def product(acc, distances, weight):
        base = {s: 8 * i for i, s in enumerate(distances)}
        spare, spared = 8 * len(distances), False
        pieces, slots = [], []
        for t in sorted({t for s in distances for t in (s, -s % 4)}):
            mine, theirs = base.get(t, spare), base.get(-t % 4, spare)
            spared |= spare in (mine, theirs)
            for other in (0, 1):
                group, part = WHERE[t, other]
                steps = [join(GROUPS[group])] + [held[f"{step}{group}"] for step in "nfc"]
                for r in range(4):
                    zz = lax.rem(z + r * sgn + 8, 4)
                    away = jnp.abs(zz // 2 - c)
                    apart = jnp.abs(jnp.abs(xl - other) - xh)
                    pieces.append((steps[r], part))
                    slots.append(mine + away * (theirs - mine) + away * 4 + apart * 2 + zz % 2)
        b_arrays = [join(names) for s in distances for names in ROWS[s]]
        return multiply(acc, pieces, slots, spare + 8 * spared, b_arrays, weight)

    acc = None
    for name, what, how, wait in STEPS:
        if isinstance(how, list):
            sent = join(what)
            if wait:
                sent = lax.optimization_barrier((sent, *(held[other] for other in wait)))[0]
            held[name] = lax.ppermute(sent, AXES, how)
        else:
            acc = held[name] = product(acc, what, how)
    return acc


def solution(mesh):
    placed = (P("row", ("layer", "col")), P(("layer", "row"), "col"))
    return jax.shard_map(
        local, mesh=mesh, in_specs=placed, out_specs=P(("row", "layer"), "col"), check_vma=False
    )
```
